32 devices in a mesh: dp: 16 (over z, y, core), tensor: 2 (over x).
Axes of the slice: x: 2, y: 2, z: 4, core: 2. Of those that a mesh axis runs over, the one named last changes fastest.
Arguments:
- prefix_kv: bfloat16 [32768, 2048], P('dp', 'tensor'), may hold values from -24 to 24
- page_key_values: bfloat16 [512, 256, 2048], P('dp', None, 'tensor'), may hold values from -6 to 6
- context_len: int32 [512], P('dp'), may hold values from 1 to 256
- prefill_owner: int32 [1], replicated, may hold values from 0 to 15
- assign: int32 [512, 1], P('dp'), may hold values from 0 to 15, as said below
- x_new: bfloat16 [512, 4, 8192], P('dp', None, 'tensor'), may hold values from -6 to 6
- norm_gain: float32 [8192], replicated, may hold values from 0.1 to 1.9
- key_weight: bfloat16 [8192, 1024], P(None, 'tensor'), may hold values from -0.25 to 0.25
- value_weight: bfloat16 [8192, 1024], P(None, 'tensor'), may hold values from -0.0625 to 0.0625
- decoded_queries: bfloat16 [512, 4, 8192], P('dp', None, 'tensor'), may hold values from -30 to 30
Outputs:
- decoded: bfloat16 [512, 4, 8192], P('dp', None, 'tensor')
The draws below stay inside these ranges and needn't reach their ends.
Inputs may be any that keep to these rules, and one draw needn't show every extreme that they name: `assign`: within the 32 requests of one device no group is named more than 2 times; one group, the same for every device, is named exactly 2 times by the requests of every device.
All inputs are finite; a program needn't handle non-finite values.
Results may differ from the reference program's by a relative error of at most 0.0088.
Values may be sent and summed in bfloat16 or wider, within the bound.
A program may use at most 192 MiB of HBM per device.

```python
import math
import jax
import jax.numpy as jnp
from jax import lax

MODEL_WIDTH = 8192
QUERY_HEADS = 64
KV_HEAD_COUNT = 8
HEAD_SIZE = 128
PAGE_POSITIONS = 256
DECODE_STEPS = 4
CAP = 2
PREFIX_TOKENS = 2048
REQUESTS_PER_DP = 32
REQUEST_TOTAL = 512
SLOTS = 32
ALL_SLOTS = 512
N_DP = 16


def draw_prefix_kv(key, part):
    key = jax.random.fold_in(key, 11)
    array_shape = (N_DP * PREFIX_TOKENS, KV_HEAD_COUNT, 2, HEAD_SIZE)
    table_entries = jnp.clip(jax.random.normal(key, array_shape, jnp.float32), -6.0, 6.0)
    return table_entries.reshape(N_DP * PREFIX_TOKENS, KV_HEAD_COUNT * 2 * HEAD_SIZE).astype(jnp.bfloat16)


def draw_decoded_queries(key, part):
    key = jax.random.fold_in(key, 23)
    array_shape = (REQUEST_TOTAL, DECODE_STEPS, QUERY_HEADS, HEAD_SIZE)
    table_entries = jnp.clip(jax.random.normal(key, array_shape, jnp.float32), -6.0, 6.0)
    return table_entries.reshape(REQUEST_TOTAL, DECODE_STEPS, QUERY_HEADS * HEAD_SIZE).astype(jnp.bfloat16)


def draw_assign(key, part):
    key = jax.random.fold_in(key, 37)
    count_of_blocks = REQUEST_TOTAL // REQUESTS_PER_DP
    busiest = jax.random.randint(jax.random.fold_in(key, 1), (), 0, N_DP).astype(jnp.int32)

    def single_block(block_key):
        first_key, second_key = jax.random.split(block_key)
        remaining = jax.random.permutation(first_key, (N_DP - 1) * CAP)[:REQUESTS_PER_DP - CAP] // CAP
        remaining = (remaining + (remaining >= busiest).astype(remaining.dtype)).astype(jnp.int32)
        listing = jnp.concatenate([jnp.zeros((CAP,), jnp.int32) + busiest, remaining])
        return jax.random.permutation(second_key, listing)
    block_keys = jax.random.split(jax.random.fold_in(key, 2), count_of_blocks)
    return jax.vmap(single_block)(block_keys).reshape(REQUEST_TOTAL, 1).astype(jnp.int32)


def place_ends(array, own_key, smallest, largest):
    spot = [jax.random.randint(jax.random.fold_in(own_key, axis), (), 0, length) for axis, length in enumerate(array.shape)]
    main_axis = array.shape.index(max(array.shape))
    next_to = spot[:main_axis] + [(spot[main_axis] + 1) % array.shape[main_axis]] + spot[main_axis + 1:]
    return array.at[tuple(spot)].set(smallest).at[tuple(next_to)].set(largest)


def block_levels(rng, extent, cuts, least, largest):
    def one(dim, shards_of):
        heights = jax.random.uniform(jax.random.fold_in(jax.random.fold_in(rng, 6), dim), (shards_of,), jnp.float32, least / len(cuts), largest / len(cuts))
        return jnp.repeat(jnp.exp(heights), extent[dim] // shards_of).reshape((-1,) + (1,) * (len(extent) - dim - 1))

    loudness = one(*cuts[0])
    for cut in cuts[1:]:
        loudness = loudness * one(*cut)
    return loudness


def scatter_about(key, shape, scale, reach, cuts=(), held_as=jnp.bfloat16):
    drawn = scale * jax.random.normal(key, shape, jnp.float32)
    if cuts:
        drawn = drawn * block_levels(key, shape, cuts, -0.22, 0.18)
    return jnp.clip(drawn, -reach, reach).astype(held_as)


def setup_inputs(seed: int = 0) -> dict:
    key_of = jax.random.split(jax.random.key(seed), 11)
    prefix_kv = draw_prefix_kv(jax.random.fold_in(key_of[10], 71), 0)
    page_key_values = scatter_about(key_of[1], (REQUEST_TOTAL, PAGE_POSITIONS, 2 * KV_HEAD_COUNT * HEAD_SIZE), 1.0, 6.0, ((0, 16), (2, 2)))
    context_len = place_ends(jax.random.randint(key_of[2], (REQUEST_TOTAL,), 1, PAGE_POSITIONS + 1), jax.random.fold_in(key_of[2], 1), 1, PAGE_POSITIONS).astype(jnp.int32)
    prefill_owner = jax.random.randint(key_of[3], (1,), 0, N_DP).astype(jnp.int32)
    assign = draw_assign(jax.random.fold_in(key_of[10], 71), 0)
    x_new = scatter_about(key_of[5], (REQUEST_TOTAL, DECODE_STEPS, MODEL_WIDTH), 1.0, 6.0, ((0, 16), (2, 2)))
    norm_gain = jnp.clip(1.0 + 0.18 * jax.random.normal(key_of[6], (MODEL_WIDTH,), jnp.float32), 0.1, 1.9)
    key_weight = scatter_about(key_of[7], (MODEL_WIDTH, KV_HEAD_COUNT * HEAD_SIZE), (MODEL_WIDTH // 16) ** -0.5, 0.25, ((1, 2),))
    value_weight = scatter_about(key_of[8], (MODEL_WIDTH, KV_HEAD_COUNT * HEAD_SIZE), MODEL_WIDTH ** -0.5, 0.0625, ((1, 2),))
    decoded_queries = draw_decoded_queries(jax.random.fold_in(key_of[10], 71), 0)
    return dict(prefix_kv=prefix_kv, page_key_values=page_key_values, context_len=context_len, prefill_owner=prefill_owner, assign=assign, x_new=x_new, norm_gain=norm_gain, key_weight=key_weight, value_weight=value_weight, decoded_queries=decoded_queries)


epsilon = 1e-05
highest_precision = lax.Precision.HIGHEST

def attend(queries, page_rows, recent_key_values, request_lengths, prefix):
    members = queries.shape[0]
    step_count = queries.shape[1]
    key_heads = prefix.shape[1] // (2 * HEAD_SIZE)
    group_size = queries.shape[2] // (key_heads * HEAD_SIZE)
    page_span = page_rows.shape[1]
    grouped = queries.astype(jnp.float32).reshape(members, step_count, key_heads, group_size, HEAD_SIZE)
    shared = prefix.astype(jnp.float32).reshape(prefix.shape[0], key_heads, 2, HEAD_SIZE)
    paged = page_rows.astype(jnp.float32).reshape(members, page_span, key_heads, 2, HEAD_SIZE)
    recent = recent_key_values.astype(jnp.float32).reshape(members, step_count, key_heads, 2, HEAD_SIZE)
    scaling = 1.0 / math.sqrt(HEAD_SIZE)
    shared_scores = jnp.einsum('ntjgd,ljd->ntjgl', grouped, shared[:, :, 0], precision=highest_precision) * scaling
    paged_scores = jnp.einsum('ntjgd,npjd->ntjgp', grouped, paged[:, :, :, 0], precision=highest_precision) * scaling
    recent_scores = jnp.einsum('ntjgd,nsjd->ntjgs', grouped, recent[:, :, :, 0], precision=highest_precision) * scaling
    position = jnp.arange(page_span).astype(jnp.float32)
    visible = position[None, :] < request_lengths[:, None]
    paged_scores = jnp.where(visible[:, None, None, None, :], paged_scores, -jnp.inf)
    causal = jnp.arange(step_count)[None, :] <= jnp.arange(step_count)[:, None]
    recent_scores = jnp.where(causal[None, :, None, None, :], recent_scores, -jnp.inf)
    highest = jnp.maximum(jnp.maximum(lax.optimization_barrier(jnp.max(shared_scores, axis=-1, keepdims=True)), lax.optimization_barrier(jnp.max(paged_scores, axis=-1, keepdims=True))), lax.optimization_barrier(jnp.max(recent_scores, axis=-1, keepdims=True)))
    shared_exp = jnp.exp(shared_scores - highest)
    paged_exp = jnp.exp(paged_scores - highest)
    recent_exp = jnp.exp(recent_scores - highest)
    denominator = lax.optimization_barrier(jnp.sum(shared_exp, axis=-1, keepdims=True)) + lax.optimization_barrier(jnp.sum(paged_exp, axis=-1, keepdims=True)) + lax.optimization_barrier(jnp.sum(recent_exp, axis=-1, keepdims=True))
    shared_weights = (shared_exp / denominator).astype(jnp.bfloat16).astype(jnp.float32)
    paged_weights = (paged_exp / denominator).astype(jnp.bfloat16).astype(jnp.float32)
    recent_weights = (recent_exp / denominator).astype(jnp.bfloat16).astype(jnp.float32)
    result = jnp.einsum('ntjgl,ljd->ntjgd', shared_weights, shared[:, :, 1], precision=highest_precision)
    result = result + jnp.einsum('ntjgp,npjd->ntjgd', paged_weights, paged[:, :, :, 1], precision=highest_precision)
    result = result + jnp.einsum('ntjgs,nsjd->ntjgd', recent_weights, recent[:, :, :, 1], precision=highest_precision)
    return result.reshape(members, step_count, key_heads * group_size * HEAD_SIZE).astype(jnp.bfloat16)

def reference(prefix_kv, page_key_values, context_len, prefill_owner, assign, x_new, norm_gain, key_weight, value_weight, decoded_queries):
    count_of_blocks = REQUEST_TOTAL // REQUESTS_PER_DP
    features = x_new.astype(jnp.float32)
    normed = (features * lax.rsqrt(lax.optimization_barrier(jnp.mean(features * features, axis=2, keepdims=True)) + epsilon) * norm_gain).astype(jnp.bfloat16)
    flattened = normed.reshape(REQUEST_TOTAL * DECODE_STEPS, MODEL_WIDTH)
    fresh_keys = jnp.dot(flattened, key_weight, preferred_element_type=jnp.float32).astype(jnp.bfloat16)
    fresh_values = jnp.dot(flattened, value_weight, preferred_element_type=jnp.float32).astype(jnp.bfloat16)
    recent_key_values = jnp.stack([fresh_keys.reshape(REQUEST_TOTAL, DECODE_STEPS, KV_HEAD_COUNT, HEAD_SIZE), fresh_values.reshape(REQUEST_TOTAL, DECODE_STEPS, KV_HEAD_COUNT, HEAD_SIZE)], axis=3).reshape(REQUEST_TOTAL, DECODE_STEPS, 2 * KV_HEAD_COUNT * HEAD_SIZE)
    start = (prefill_owner[0] * PREFIX_TOKENS).astype(jnp.int32)
    prefix = lax.dynamic_slice_in_dim(prefix_kv, start, PREFIX_TOKENS, 0)
    request_lengths = context_len.astype(jnp.float32)

    def single_block(pieces):
        return attend(pieces[0], pieces[1], pieces[2], pieces[3], prefix)
    attended_output = lax.map(single_block, (decoded_queries.reshape(count_of_blocks, REQUESTS_PER_DP, DECODE_STEPS, QUERY_HEADS * HEAD_SIZE), page_key_values.reshape(count_of_blocks, REQUESTS_PER_DP, PAGE_POSITIONS, 2 * KV_HEAD_COUNT * HEAD_SIZE), recent_key_values.reshape(count_of_blocks, REQUESTS_PER_DP, DECODE_STEPS, 2 * KV_HEAD_COUNT * HEAD_SIZE), request_lengths.reshape(count_of_blocks, REQUESTS_PER_DP)))
    attended_output = attended_output.reshape(REQUEST_TOTAL, DECODE_STEPS, QUERY_HEADS * HEAD_SIZE)
    assigned = assign[:, 0].reshape(count_of_blocks, REQUESTS_PER_DP)
    indices = jnp.arange(REQUESTS_PER_DP)
    matching = (assigned[:, :, None] == assigned[:, None, :]) & (indices[None, None, :] < indices[None, :, None])
    ranking = lax.optimization_barrier(jnp.sum(matching.astype(jnp.int32), axis=2))
    slot_index = assigned * SLOTS + jnp.arange(count_of_blocks).astype(jnp.int32)[:, None] * CAP + ranking
    decoded = jnp.zeros((ALL_SLOTS, DECODE_STEPS, QUERY_HEADS * HEAD_SIZE), jnp.bfloat16).at[slot_index.reshape(REQUEST_TOTAL).astype(jnp.int32)].set(attended_output)
    return decoded
```

```python
import functools
import math

import jax
import jax.numpy as jnp
from jax import lax
from jax.experimental import pallas as pl
from jax.experimental.pallas import tpu as pltpu
from jax.sharding import PartitionSpec as P

HEAD_SIZE = 128
CAP = 2
epsilon = 1e-05
SCALE2 = math.log2(math.e) / math.sqrt(HEAD_SIZE)
VMEM_LIMIT = 56 * 1024 * 1024
NT = (((1,), (1,)), ((), ()))


def broadcast(block, axis, holder):
    block = jnp.where(lax.axis_index(axis) == holder, block, jnp.zeros_like(block))
    return lax.psum(block, axis)


def page_kernel(key_heads, group, steps, span, len_ref, q_ref, page_ref, acc_ref, top_ref, sum_ref):
    i = pl.program_id(0)
    tile = q_ref.shape[0]
    per_pair = 8 // steps
    queries = q_ref[...].astype(jnp.float32)
    rows = group * 8
    keys = per_pair * span
    row = lax.broadcasted_iota(jnp.int32, (rows, keys), 0)
    col = lax.broadcasted_iota(jnp.int32, (rows, keys), 1)
    owner = (row % 8) // steps
    for p in range(tile // 8):
        limit = jnp.zeros((rows, keys), jnp.int32)
        for k in range(per_pair):
            used = len_ref[i * (tile // steps) + p * per_pair + k]
            limit = jnp.where(owner == k, used, limit)
        place = col - owner * span
        visible = (place >= 0) & (place < limit)
        base = p * per_pair
        for j in range(key_heads):
            q = jnp.concatenate(
                [
                    queries[p * 8 : p * 8 + 8, (j * group + g) * HEAD_SIZE : (j * group + g + 1) * HEAD_SIZE]
                    for g in range(group)
                ],
                axis=0,
            ).astype(jnp.bfloat16)
            c = 2 * j * HEAD_SIZE
            k = page_ref[base : base + per_pair, :, c : c + HEAD_SIZE].reshape(keys, HEAD_SIZE)
            v = page_ref[base : base + per_pair, :, c + HEAD_SIZE : c + 2 * HEAD_SIZE].reshape(keys, HEAD_SIZE)
            s = lax.dot_general(q, k, NT, preferred_element_type=jnp.float32)
            s = jnp.where(visible, s, -jnp.inf)
            top = jnp.max(s, axis=1, keepdims=True)
            e = jnp.exp2((s - top) * SCALE2)
            total = jnp.sum(e, axis=1, keepdims=True)
            acc = jnp.dot(e.astype(jnp.bfloat16), v, preferred_element_type=jnp.float32)
            top = jnp.broadcast_to(top, acc.shape)
            total = jnp.broadcast_to(total, acc.shape)
            for g in range(group):
                acc_ref[j, g, p * 8 : p * 8 + 8, :] = acc[g * 8 : g * 8 + 8]
                top_ref[j, g, p * 8 : p * 8 + 8, :] = top[g * 8 : g * 8 + 8]
                sum_ref[j, g, p * 8 : p * 8 + 8, :] = total[g * 8 : g * 8 + 8]


def page_part(queries, pages, lengths, steps):
    tokens, width = queries.shape
    members, span, kv_width = pages.shape
    key_heads = kv_width // (2 * HEAD_SIZE)
    group = width // (key_heads * HEAD_SIZE)
    tile = 16
    grid = tokens // tile
    shape = jax.ShapeDtypeStruct((key_heads, group, tokens, HEAD_SIZE), jnp.float32)
    spec = pl.BlockSpec((key_heads, group, tile, HEAD_SIZE), lambda i: (0, 0, i, 0))
    return pl.pallas_call(
        functools.partial(page_kernel, key_heads, group, steps, span),
        grid=(grid,),
        in_specs=[
            pl.BlockSpec(memory_space=pltpu.SMEM),
            pl.BlockSpec((tile, width), lambda i: (i, 0)),
            pl.BlockSpec((tile // steps, span, kv_width), lambda i: (i, 0, 0)),
        ],
        out_specs=[spec] * 3,
        out_shape=[shape] * 3,
        compiler_params=pltpu.CompilerParams(vmem_limit_bytes=VMEM_LIMIT),
        cost_estimate=pl.CostEstimate(
            flops=16 * tokens * span * width, bytes_accessed=2 * pages.size, transcendentals=0
        ),
    )(lengths, queries, pages)


def prefix_kernel(group, steps, q_ref, kv_ref, nk_ref, nv_ref, acc_ref, top_ref, sum_ref, out_ref):
    tokens = q_ref.shape[0]
    keys = kv_ref[:, :HEAD_SIZE]
    values = kv_ref[:, HEAD_SIZE:]
    wide = 2
    row = lax.broadcasted_iota(jnp.int32, (wide * tokens, tokens), 0) % tokens
    col = lax.broadcasted_iota(jnp.int32, (wide * tokens, tokens), 1)
    visible = (row // steps == col // steps) & (col <= row)
    for g in range(0, group, wide):
        q = jnp.concatenate(
            [q_ref[:, (g + w) * HEAD_SIZE : (g + w + 1) * HEAD_SIZE] for w in range(wide)], axis=0
        )
        paged = jnp.concatenate([acc_ref[0, g + w] for w in range(wide)], axis=0)
        paged_top = jnp.concatenate([top_ref[0, g + w][:, :1] for w in range(wide)], axis=0)
        paged_sum = jnp.concatenate([sum_ref[0, g + w][:, :1] for w in range(wide)], axis=0)
        s = lax.dot_general(q, keys, NT, preferred_element_type=jnp.float32)
        r = lax.dot_general(q, nk_ref[...], NT, preferred_element_type=jnp.float32)
        r = jnp.where(visible, r, -jnp.inf)
        top = jnp.maximum(jnp.max(s, axis=1, keepdims=True), jnp.max(r, axis=1, keepdims=True))
        top = jnp.maximum(top, paged_top)
        e = jnp.exp2((s - top) * SCALE2)
        f = jnp.exp2((r - top) * SCALE2)
        keep = jnp.exp2((paged_top - top) * SCALE2)
        total = (
            jnp.sum(e, axis=1, keepdims=True) + jnp.sum(f, axis=1, keepdims=True) + keep * paged_sum
        )
        acc = jnp.dot(e.astype(jnp.bfloat16), values, preferred_element_type=jnp.float32)
        acc += jnp.dot(f.astype(jnp.bfloat16), nv_ref[...], preferred_element_type=jnp.float32)
        acc = (acc + keep * paged) / total
        for w in range(wide):
            out_ref[:, (g + w) * HEAD_SIZE : (g + w + 1) * HEAD_SIZE] = acc[
                w * tokens : (w + 1) * tokens
            ].astype(jnp.bfloat16)


def prefix_part(queries, prefix, new_keys, new_values, paged, steps):
    tokens, width = queries.shape
    length, kv_width = prefix.shape
    key_heads = kv_width // (2 * HEAD_SIZE)
    group = width // (key_heads * HEAD_SIZE)
    part = pl.BlockSpec((1, group, tokens, HEAD_SIZE), lambda j: (j, 0, 0, 0))
    return pl.pallas_call(
        functools.partial(prefix_kernel, group, steps),
        grid=(key_heads,),
        in_specs=[
            pl.BlockSpec((tokens, group * HEAD_SIZE), lambda j: (0, j)),
            pl.BlockSpec((length, 2 * HEAD_SIZE), lambda j: (0, j)),
            pl.BlockSpec((tokens, HEAD_SIZE), lambda j: (0, j)),
            pl.BlockSpec((tokens, HEAD_SIZE), lambda j: (0, j)),
            part,
            part,
            part,
        ],
        out_specs=pl.BlockSpec((tokens, group * HEAD_SIZE), lambda j: (0, j)),
        out_shape=jax.ShapeDtypeStruct((tokens, width), jnp.bfloat16),
        compiler_params=pltpu.CompilerParams(vmem_limit_bytes=VMEM_LIMIT),
        cost_estimate=pl.CostEstimate(
            flops=4 * tokens * length * width, bytes_accessed=2 * prefix.size, transcendentals=0
        ),
    )(queries, prefix, new_keys, new_values, *paged)


def per_device(
    prefix_kv,
    page_key_values,
    context_len,
    prefill_owner,
    assign,
    x_new,
    norm_gain,
    key_weight,
    value_weight,
    decoded_queries,
):
    row_count, step_count, width = decoded_queries.shape
    tokens = row_count * step_count
    prefix = broadcast(prefix_kv, "dp", prefill_owner[0])
    features = lax.all_gather(x_new, "tensor", axis=2, tiled=True).astype(jnp.float32)
    normed = (
        features
        * lax.rsqrt(jnp.mean(features * features, axis=2, keepdims=True) + epsilon)
        * norm_gain
    ).astype(jnp.bfloat16)
    flattened = normed.reshape(tokens, features.shape[2])
    new_keys = jnp.dot(flattened, key_weight, preferred_element_type=jnp.float32).astype(jnp.bfloat16)
    new_values = jnp.dot(flattened, value_weight, preferred_element_type=jnp.float32).astype(
        jnp.bfloat16
    )
    queries = decoded_queries.reshape(tokens, width)
    paged = page_part(queries, page_key_values, context_len, step_count)
    attended = prefix_part(queries, prefix, new_keys, new_values, paged, step_count)

    group_count = lax.axis_size("dp")
    assigned = assign[:, 0]
    indices = jnp.arange(row_count)
    matching = (assigned[:, None] == assigned[None, :]) & (indices[None, :] < indices[:, None])
    ranking = jnp.sum(matching.astype(jnp.int32), axis=1)
    destination = assigned * CAP + ranking
    selector = (jnp.arange(group_count * CAP)[:, None] == destination[None, :]).astype(jnp.bfloat16)
    arranged = jnp.dot(
        selector, attended.reshape(row_count, -1), preferred_element_type=jnp.bfloat16
    ).reshape(group_count, CAP, step_count, width)
    decoded = lax.all_to_all(arranged, "dp", split_axis=0, concat_axis=0, tiled=True)
    return decoded.reshape(group_count * CAP, step_count, width)


def solution(mesh):
    in_specs = (
        P("dp", "tensor"),
        P("dp", None, "tensor"),
        P("dp"),
        P(),
        P("dp", None),
        P("dp", None, "tensor"),
        P(),
        P(None, "tensor"),
        P(None, "tensor"),
        P("dp", None, "tensor"),
    )
    out_specs = P("dp", None, "tensor")
    return jax.shard_map(
        per_device, mesh=mesh, in_specs=in_specs, out_specs=out_specs, check_vma=False
    )
```

```python
import functools
import math

import jax
import jax.numpy as jnp
from jax import lax
from jax.experimental import pallas as pl
from jax.experimental.pallas import tpu as pltpu
from jax.sharding import PartitionSpec as P

HEAD_SIZE = 128
CAP = 2
epsilon = 1e-05
SCALE2 = math.log2(math.e) / math.sqrt(HEAD_SIZE)
VMEM_LIMIT = 56 * 1024 * 1024
NT = (((1,), (1,)), ((), ()))


def bit(index, b):
    return (index // 2**b) % 2


def kernel(
    steps,
    levels,
    ranks,
    len_ref,
    owner_ref,
    q_ref,
    page_ref,
    x_ref,
    gain_ref,
    wk_ref,
    wv_ref,
    sel_ref,
    prefix_ref,
    out_ref,
    work,
    full,
    x_all,
    acc_ref,
    top_ref,
    sum_ref,
    nk_sum,
    nv_sum,
    square_sum,
    nk_ref,
    nv_ref,
    outgoing,
    copy_sem,
    send_sem,
    recv_sem,
    x_send,
    x_recv,
    o_send,
    o_recv,
    own_sem,
    *landing,
):
    i = pl.program_id(0)
    me = lax.axis_index("dp")
    rank = lax.axis_index("tensor")
    members = 2**levels
    tokens, width = q_ref.shape
    length = prefix_ref.shape[0]
    key_heads = work.shape[0]
    group = width // (key_heads * HEAD_SIZE)
    span = page_ref.shape[1]
    page_steps = tokens // 16
    chunks, _, chunk = gain_ref.shape
    own_chunks = chunks // ranks
    head_width = group * HEAD_SIZE
    final_step = page_steps + chunks + key_heads - 1
    stages = 2 * levels

    def low(b, first):
        start = 0
        for a in range(first, b + 1):
            start = start + bit(me, a) * (length >> (a + 1))
        return start

    def rows(start, size):
        return pl.ds(pl.multiple_of(start, size), size)

    def transfer(k, j):
        if k < levels:
            b = k
            size = length >> (b + 1)
            if b == 0:
                start = (1 - bit(me, 0)) * size
                source = prefix_ref.at[rows(start, size), j * 2 * HEAD_SIZE : (j + 1) * 2 * HEAD_SIZE]
            else:
                start = low(b - 1, 1) + (1 - bit(me, b)) * size
                source = work.at[j, rows(start, size), :]
            target = landing[b].at[j]
        else:
            b = stages - 1 - k
            size = length >> (b + 1)
            source = full.at[j, rows(low(b, 0), size), :]
            target = source
        partner = me + (1 - 2 * bit(me, b)) * 2**b
        return pltpu.make_async_remote_copy(
            src_ref=source,
            dst_ref=target,
            send_sem=send_sem.at[k, j],
            recv_sem=recv_sem.at[k, j],
            device_id={"dp": partner},
            device_id_type=pl.DeviceIdType.MESH,
        )

    def kept(j):
        size = length // 2
        return pltpu.make_async_copy(
            prefix_ref.at[rows(bit(me, 0) * size, size), j * 2 * HEAD_SIZE : (j + 1) * 2 * HEAD_SIZE],
            work.at[j],
            copy_sem.at[j],
        )

    def x_transfer(p, c):
        peer = lax.rem(rank + p, ranks)
        return pltpu.make_async_remote_copy(
            src_ref=x_ref.at[:, c * chunk : (c + 1) * chunk],
            dst_ref=x_all.at[rank * own_chunks + c],
            send_sem=x_send.at[p - 1, c],
            recv_sem=x_recv.at[p - 1, c],
            device_id={"tensor": peer},
            device_id_type=pl.DeviceIdType.MESH,
        )

    def out_transfer(j, p):
        dest = lax.rem(me + p, members)
        return pltpu.make_async_remote_copy(
            src_ref=outgoing.at[j, dest],
            dst_ref=out_ref.at[me, :, j * head_width : (j + 1) * head_width],
            send_sem=o_send.at[j, p],
            recv_sem=o_recv.at[j, p],
            device_id={"dp": dest},
            device_id_type=pl.DeviceIdType.MESH,
        )

    def own_out(j):
        return pltpu.make_async_copy(
            outgoing.at[j, me],
            out_ref.at[me, :, j * head_width : (j + 1) * head_width],
            own_sem.at[j],
        )

    def advance(k, j):
        transfer(k, j).wait_recv()
        if k < levels:
            b = k
            size = length >> (b + 1)
            if b == 0:
                kept(j).wait()
            span_rows = rows(low(b, 1), size)
            mine = work[j, span_rows, :]
            other = landing[b][j]
            side = jnp.zeros(mine.shape, jnp.int32) + owner_ref[0]
            away = ((side // 2**b) % 2 - bit(me, b)).astype(jnp.float32)
            away = (away * away).astype(jnp.bfloat16)
            merged = mine * (1 - away) + other * away
            if b < levels - 1:
                work[j, span_rows, :] = merged
            else:
                full[j, rows(low(b, 0), size), :] = merged
        if k < stages - 1:
            transfer(k + 1, j).start()

    @pl.when(i == 0)
    def _():
        barrier = pltpu.get_barrier_semaphore()

        def greet(p, carry):
            pl.semaphore_signal(
                barrier,
                inc=1,
                device_id={"dp": lax.rem(me + p, members)},
                device_id_type=pl.DeviceIdType.MESH,
            )
            return carry

        lax.fori_loop(1, members, greet, 0)
        for p in range(1, ranks):
            pl.semaphore_signal(
                barrier,
                inc=1,
                device_id={"tensor": lax.rem(rank + p, ranks)},
                device_id_type=pl.DeviceIdType.MESH,
            )
        for j in range(key_heads):
            kept(j).start()
        pl.semaphore_wait(barrier, members - 1 + ranks - 1)
        for j in range(key_heads):
            transfer(0, j).start()
        for p in range(1, ranks):
            for c in range(own_chunks):
                x_transfer(p, c).start()
        for c in range(own_chunks):
            x_all[rank * own_chunks + c] = x_ref[:, c * chunk : (c + 1) * chunk]
        nk_sum[...] = jnp.zeros_like(nk_sum)
        nv_sum[...] = jnp.zeros_like(nv_sum)
        square_sum[...] = jnp.zeros_like(square_sum)

    @pl.when(i < page_steps)
    def _():
        per_pair = 8 // steps
        queries = q_ref[pl.ds(pl.multiple_of(i * 16, 16), 16), :].astype(jnp.float32)
        count = group * 8
        keys = per_pair * span
        row = lax.broadcasted_iota(jnp.int32, (count, keys), 0)
        col = lax.broadcasted_iota(jnp.int32, (count, keys), 1)
        holder = (row % 8) // steps
        for p in range(2):
            limit = jnp.zeros((count, keys), jnp.int32)
            for k in range(per_pair):
                used = len_ref[i * (16 // steps) + p * per_pair + k]
                limit = jnp.where(holder == k, used, limit)
            place = col - holder * span
            visible = (place >= 0) & (place < limit)
            base = p * per_pair
            spot = pl.ds(pl.multiple_of(i * 16 + p * 8, 8), 8)
            for j in range(key_heads):
                q = jnp.concatenate(
                    [
                        queries[
                            p * 8 : p * 8 + 8,
                            (j * group + g) * HEAD_SIZE : (j * group + g + 1) * HEAD_SIZE,
                        ]
                        for g in range(group)
                    ],
                    axis=0,
                ).astype(jnp.bfloat16)
                c = 2 * j * HEAD_SIZE
                k = page_ref[base : base + per_pair, :, c : c + HEAD_SIZE].reshape(keys, HEAD_SIZE)
                v = page_ref[base : base + per_pair, :, c + HEAD_SIZE : c + 2 * HEAD_SIZE]
                v = v.reshape(keys, HEAD_SIZE)
                s = lax.dot_general(q, k, NT, preferred_element_type=jnp.float32)
                s = jnp.where(visible, s, -jnp.inf)
                top = jnp.max(s, axis=1, keepdims=True)
                e = jnp.exp2((s - top) * SCALE2)
                total = jnp.sum(e, axis=1, keepdims=True)
                acc = jnp.dot(e.astype(jnp.bfloat16), v, preferred_element_type=jnp.float32)
                top = jnp.broadcast_to(top, acc.shape)
                total = jnp.broadcast_to(total, acc.shape)
                for g in range(group):
                    acc_ref[j, g, spot, :] = acc[g * 8 : g * 8 + 8]
                    top_ref[j, g, spot, :] = top[g * 8 : g * 8 + 8]
                    sum_ref[j, g, spot, :] = total[g * 8 : g * 8 + 8]

    @pl.when(i == page_steps)
    def _():
        for p in range(1, ranks):
            for c in range(own_chunks):
                x_transfer(p, c).wait()

    @pl.when((i >= page_steps) & (i < page_steps + chunks))
    def _():
        c = i - page_steps
        x = x_all[c].astype(jnp.float32)
        square_sum[...] += jnp.sum(x * x, axis=1, keepdims=True)
        scaled = (x * gain_ref[c]).astype(jnp.bfloat16)
        nk_sum[...] += jnp.dot(scaled, wk_ref[...], preferred_element_type=jnp.float32)
        nv_sum[...] += jnp.dot(scaled, wv_ref[...], preferred_element_type=jnp.float32)

    @pl.when(i == page_steps + chunks - 1)
    def _():
        inverse = lax.rsqrt(square_sum[:, :1] / (chunks * chunk) + epsilon)
        nk = (nk_sum[...] * inverse).astype(jnp.bfloat16)
        nv = (nv_sum[...] * inverse).astype(jnp.bfloat16)
        for j in range(key_heads):
            nk_ref[j] = nk[:, j * HEAD_SIZE : (j + 1) * HEAD_SIZE]
            nv_ref[j] = nv[:, j * HEAD_SIZE : (j + 1) * HEAD_SIZE]

    def attend(j):
        keys = full[j, :, :HEAD_SIZE]
        values = full[j, :, HEAD_SIZE:]
        wide = 2
        row = lax.broadcasted_iota(jnp.int32, (wide * tokens, tokens), 0) % tokens
        col = lax.broadcasted_iota(jnp.int32, (wide * tokens, tokens), 1)
        visible = (row // steps == col // steps) & (col <= row)
        for g in range(0, group, wide):
            first = j * head_width + g * HEAD_SIZE
            q = jnp.concatenate(
                [
                    q_ref[:, first + w * HEAD_SIZE : first + (w + 1) * HEAD_SIZE]
                    for w in range(wide)
                ],
                axis=0,
            )
            paged = jnp.concatenate([acc_ref[j, g + w] for w in range(wide)], axis=0)
            paged_top = jnp.concatenate([top_ref[j, g + w][:, :1] for w in range(wide)], axis=0)
            paged_sum = jnp.concatenate([sum_ref[j, g + w][:, :1] for w in range(wide)], axis=0)
            s = lax.dot_general(q, keys, NT, preferred_element_type=jnp.float32)
            r = lax.dot_general(q, nk_ref[j], NT, preferred_element_type=jnp.float32)
            r = jnp.where(visible, r, -jnp.inf)
            top = jnp.maximum(jnp.max(s, axis=1, keepdims=True), jnp.max(r, axis=1, keepdims=True))
            top = jnp.maximum(top, paged_top)
            e = jnp.exp2((s - top) * SCALE2)
            f = jnp.exp2((r - top) * SCALE2)
            keep = jnp.exp2((paged_top - top) * SCALE2)
            total = (
                jnp.sum(e, axis=1, keepdims=True)
                + jnp.sum(f, axis=1, keepdims=True)
                + keep * paged_sum
            )
            acc = jnp.dot(e.astype(jnp.bfloat16), values, preferred_element_type=jnp.float32)
            acc += jnp.dot(f.astype(jnp.bfloat16), nv_ref[j], preferred_element_type=jnp.float32)
            acc = ((acc + keep * paged) / total).astype(jnp.bfloat16)
            both = jnp.concatenate([acc[w * tokens : (w + 1) * tokens] for w in range(wide)], axis=1)
            placed = jnp.dot(sel_ref[...], both, preferred_element_type=jnp.float32)
            outgoing[j, :, :, g * HEAD_SIZE : (g + wide) * HEAD_SIZE] = placed.reshape(
                members, CAP * steps, wide * HEAD_SIZE
            ).astype(jnp.bfloat16)

    for j in range(key_heads):

        @pl.when(i == page_steps + chunks + j)
        def _(j=j):
            attend(j)

            def send(p, carry):
                out_transfer(j, p).start()
                return carry

            lax.fori_loop(1, members, send, 0)
            own_out(j).start()

    for t in range(stages + key_heads - 1):
        if t < page_steps:
            when = t
        else:
            when = page_steps + (t - page_steps) * 4 + 1

        @pl.when(i == when)
        def _(t=t):
            for j in range(key_heads):
                if 0 <= t - j < stages:
                    advance(t - j, j)

    @pl.when(i == final_step)
    def _():
        for j in range(key_heads):
            for k in range(stages):
                transfer(k, j).wait_send()

            def finish(p, carry):
                out_transfer(j, p).wait()
                return carry

            lax.fori_loop(1, members, finish, 0)
            own_out(j).wait()


def per_device(
    prefix_kv,
    page_key_values,
    context_len,
    prefill_owner,
    assign,
    x_new,
    norm_gain,
    key_weight,
    value_weight,
    decoded_queries,
):
    row_count, steps, width = decoded_queries.shape
    tokens = row_count * steps
    members = lax.axis_size("dp")
    ranks = lax.axis_size("tensor")
    levels = members.bit_length() - 1
    assigned = assign[:, 0]
    indices = jnp.arange(row_count)
    matching = (assigned[:, None] == assigned[None, :]) & (indices[None, :] < indices[:, None])
    ranking = jnp.sum(matching.astype(jnp.int32), axis=1)
    destination = assigned * CAP + ranking
    token_place = (destination[:, None] * steps + jnp.arange(steps)[None, :]).reshape(tokens)
    slots = members * CAP * steps
    selector = (jnp.arange(slots)[:, None] == token_place[None, :]).astype(jnp.bfloat16)

    length, kv_width = prefix_kv.shape
    span = page_key_values.shape[1]
    key_heads = kv_width // (2 * HEAD_SIZE)
    group = width // (key_heads * HEAD_SIZE)
    chunk = min(1024, width)
    chunks = ranks * width // chunk
    page_steps = tokens // 16
    new_width = key_weight.shape[1]

    def whole(*shape):
        return pl.BlockSpec(shape, lambda i: (0,) * len(shape))

    weight = pl.BlockSpec((chunk, new_width), lambda i: (jnp.clip(i - page_steps, 0, chunks - 1), 0))
    stat = pltpu.VMEM((key_heads, group, tokens, HEAD_SIZE), jnp.float32)
    decoded = pl.pallas_call(
        functools.partial(kernel, steps, levels, ranks),
        grid=(page_steps + chunks + key_heads,),
        in_specs=[
            pl.BlockSpec(memory_space=pltpu.SMEM),
            pl.BlockSpec(memory_space=pltpu.SMEM),
            whole(tokens, width),
            pl.BlockSpec(
                (16 // steps, span, kv_width), lambda i: (jnp.minimum(i, page_steps - 1), 0, 0)
            ),
            whole(tokens, width),
            whole(chunks, 1, chunk),
            weight,
            weight,
            whole(slots, tokens),
            pl.BlockSpec(memory_space=pl.ANY),
        ],
        out_specs=pl.BlockSpec(memory_space=pl.ANY),
        out_shape=jax.ShapeDtypeStruct((members, CAP * steps, width), jnp.bfloat16),
        scratch_shapes=[
            pltpu.VMEM((key_heads, length // 2, 2 * HEAD_SIZE), jnp.bfloat16),
            pltpu.VMEM((key_heads, length, 2 * HEAD_SIZE), jnp.bfloat16),
            pltpu.VMEM((chunks, tokens, chunk), jnp.bfloat16),
            stat,
            stat,
            stat,
            pltpu.VMEM((tokens, new_width), jnp.float32),
            pltpu.VMEM((tokens, new_width), jnp.float32),
            pltpu.VMEM((tokens, HEAD_SIZE), jnp.float32),
            pltpu.VMEM((key_heads, tokens, HEAD_SIZE), jnp.bfloat16),
            pltpu.VMEM((key_heads, tokens, HEAD_SIZE), jnp.bfloat16),
            pltpu.VMEM((key_heads, members, CAP * steps, group * HEAD_SIZE), jnp.bfloat16),
            pltpu.SemaphoreType.DMA((key_heads,)),
            pltpu.SemaphoreType.DMA((2 * levels, key_heads)),
            pltpu.SemaphoreType.DMA((2 * levels, key_heads)),
            pltpu.SemaphoreType.DMA((ranks - 1, width // chunk)),
            pltpu.SemaphoreType.DMA((ranks - 1, width // chunk)),
            pltpu.SemaphoreType.DMA((key_heads, members)),
            pltpu.SemaphoreType.DMA((key_heads, members)),
            pltpu.SemaphoreType.DMA((key_heads,)),
        ]
        + [
            pltpu.VMEM((key_heads, length >> (b + 1), 2 * HEAD_SIZE), jnp.bfloat16)
            for b in range(levels)
        ],
        compiler_params=pltpu.CompilerParams(
            collective_id=0,
            has_side_effects=True,
            vmem_limit_bytes=VMEM_LIMIT,
            dimension_semantics=("arbitrary",),
        ),
        cost_estimate=pl.CostEstimate(
            flops=4 * tokens * length * width, bytes_accessed=2 * page_key_values.size, transcendentals=0
        ),
    )(
        context_len,
        prefill_owner,
        decoded_queries.reshape(tokens, width),
        page_key_values,
        x_new.reshape(tokens, width),
        norm_gain.reshape(chunks, 1, chunk),
        key_weight,
        value_weight,
        selector,
        prefix_kv,
    )
    return decoded.reshape(members * CAP, steps, width)


def solution(mesh):
    in_specs = (
        P("dp", "tensor"),
        P("dp", None, "tensor"),
        P("dp"),
        P(),
        P("dp", None),
        P("dp", None, "tensor"),
        P(),
        P(None, "tensor"),
        P(None, "tensor"),
        P("dp", None, "tensor"),
    )
    out_specs = P("dp", None, "tensor")
    return jax.shard_map(
        per_device, mesh=mesh, in_specs=in_specs, out_specs=out_specs, check_vma=False
    )
```

```python
import functools
import math

import jax
import jax.numpy as jnp
from jax import lax
from jax.experimental import pallas as pl
from jax.experimental.pallas import tpu as pltpu
from jax.sharding import PartitionSpec as P

HEAD_SIZE = 128
CAP = 2
epsilon = 1e-05
SCALE2 = math.log2(math.e) / math.sqrt(HEAD_SIZE)
VMEM_LIMIT = 56 * 1024 * 1024
NT = (((1,), (1,)), ((), ()))


def bit(index, b):
    return (index // 2**b) % 2


def kernel(
    steps,
    levels,
    ranks,
    len_ref,
    owner_ref,
    q_in,
    page_ref,
    x_ref,
    gain_ref,
    wk_ref,
    wv_ref,
    sel_ref,
    prefix_ref,
    out_ref,
    q_ref,
    work,
    full,
    x_all,
    acc_ref,
    top_ref,
    sum_ref,
    nk_sum,
    nv_sum,
    inverse_ref,
    nk_ref,
    nv_ref,
    outgoing,
    copy_sem,
    send_sem,
    recv_sem,
    x_send,
    x_recv,
    o_send,
    o_recv,
    own_sem,
    *landing,
):
    i = pl.program_id(0)
    me = lax.axis_index("dp")
    rank = lax.axis_index("tensor")
    members = 2**levels
    tokens, width = q_ref.shape
    length = prefix_ref.shape[0]
    key_heads = work.shape[0]
    group = width // (key_heads * HEAD_SIZE)
    span = page_ref.shape[1]
    page_steps = tokens // 16
    chunks, _, chunk = gain_ref.shape
    own_chunks = chunks // ranks
    head_width = group * HEAD_SIZE
    final_step = page_steps + chunks + key_heads - 1
    stages = 2 * levels

    def flat(block):
        return block.astype(jnp.float32).reshape(tokens, block.shape[-1])

    def low(b, first):
        start = 0
        for a in range(first, b + 1):
            start = start + bit(me, a) * (length >> (a + 1))
        return start

    def rows(start, size):
        return pl.ds(pl.multiple_of(start, size), size)

    def transfer(k, j):
        if k < levels:
            b = k
            size = length >> (b + 1)
            if b == 0:
                start = (1 - bit(me, 0)) * size
                source = prefix_ref.at[rows(start, size), j * 2 * HEAD_SIZE : (j + 1) * 2 * HEAD_SIZE]
            else:
                start = low(b - 1, 1) + (1 - bit(me, b)) * size
                source = work.at[j, rows(start, size), :]
            target = landing[b].at[j]
        else:
            b = stages - 1 - k
            size = length >> (b + 1)
            source = full.at[j, rows(low(b, 0), size), :]
            target = source
        partner = me + (1 - 2 * bit(me, b)) * 2**b
        return pltpu.make_async_remote_copy(
            src_ref=source,
            dst_ref=target,
            send_sem=send_sem.at[k, j],
            recv_sem=recv_sem.at[k, j],
            device_id={"dp": partner},
            device_id_type=pl.DeviceIdType.MESH,
        )

    def kept(j):
        size = length // 2
        return pltpu.make_async_copy(
            prefix_ref.at[rows(bit(me, 0) * size, size), j * 2 * HEAD_SIZE : (j + 1) * 2 * HEAD_SIZE],
            work.at[j],
            copy_sem.at[j],
        )

    def x_transfer(p, c):
        peer = lax.rem(rank + p, ranks)
        return pltpu.make_async_remote_copy(
            src_ref=x_ref.at[:, :, c * chunk : (c + 1) * chunk],
            dst_ref=x_all.at[rank * own_chunks + c],
            send_sem=x_send.at[p - 1, c],
            recv_sem=x_recv.at[p - 1, c],
            device_id={"tensor": peer},
            device_id_type=pl.DeviceIdType.MESH,
        )

    def out_transfer(j, p):
        dest = lax.rem(me + p, members)
        return pltpu.make_async_remote_copy(
            src_ref=outgoing.at[j, dest],
            dst_ref=out_ref.at[pl.ds(me * CAP, CAP), :, j * head_width : (j + 1) * head_width],
            send_sem=o_send.at[j, p],
            recv_sem=o_recv.at[j, p],
            device_id={"dp": dest},
            device_id_type=pl.DeviceIdType.MESH,
        )

    def own_out(j):
        return pltpu.make_async_copy(
            outgoing.at[j, me],
            out_ref.at[pl.ds(me * CAP, CAP), :, j * head_width : (j + 1) * head_width],
            own_sem.at[j],
        )

    def advance(k, j):
        transfer(k, j).wait_recv()
        if k < levels:
            b = k
            size = length >> (b + 1)
            if b == 0:
                kept(j).wait()
            span_rows = rows(low(b, 1), size)
            mine = work[j, span_rows, :]
            other = landing[b][j]
            side = jnp.zeros(mine.shape, jnp.int32) + owner_ref[0]
            away = ((side // 2**b) % 2 - bit(me, b)).astype(jnp.float32)
            away = (away * away).astype(jnp.bfloat16)
            merged = mine * (1 - away) + other * away
            if b < levels - 1:
                work[j, span_rows, :] = merged
            else:
                full[j, rows(low(b, 0), size), :] = merged
        if k < stages - 1:
            transfer(k + 1, j).start()

    @pl.when(i == 0)
    def _():
        barrier = pltpu.get_barrier_semaphore()

        def greet(p, carry):
            pl.semaphore_signal(
                barrier,
                inc=1,
                device_id={"dp": lax.rem(me + p, members)},
                device_id_type=pl.DeviceIdType.MESH,
            )
            return carry

        lax.fori_loop(1, members, greet, 0)
        for p in range(1, ranks):
            pl.semaphore_signal(
                barrier,
                inc=1,
                device_id={"tensor": lax.rem(rank + p, ranks)},
                device_id_type=pl.DeviceIdType.MESH,
            )
        for j in range(key_heads):
            kept(j).start()
        pl.semaphore_wait(barrier, members - 1 + ranks - 1)
        for j in range(key_heads):
            transfer(0, j).start()
        for p in range(1, ranks):
            for c in range(own_chunks):
                x_transfer(p, c).start()
        for c in range(own_chunks):
            x_all[rank * own_chunks + c] = x_ref[:, :, c * chunk : (c + 1) * chunk]
        for c in range(own_chunks):
            q_ref[:, c * chunk : (c + 1) * chunk] = flat(
                q_in[:, :, c * chunk : (c + 1) * chunk]
            ).astype(jnp.bfloat16)
        nk_sum[...] = jnp.zeros_like(nk_sum)
        nv_sum[...] = jnp.zeros_like(nv_sum)

    @pl.when(i < page_steps)
    def _():
        per_pair = 8 // steps
        queries = q_ref[pl.ds(pl.multiple_of(i * 16, 16), 16), :].astype(jnp.float32)
        count = group * 8
        keys = per_pair * span
        row = lax.broadcasted_iota(jnp.int32, (count, keys), 0)
        col = lax.broadcasted_iota(jnp.int32, (count, keys), 1)
        holder = (row % 8) // steps
        for p in range(2):
            limit = jnp.zeros((count, keys), jnp.int32)
            for k in range(per_pair):
                used = len_ref[i * (16 // steps) + p * per_pair + k]
                limit = jnp.where(holder == k, used, limit)
            place = col - holder * span
            visible = (place >= 0) & (place < limit)
            base = p * per_pair
            spot = pl.ds(pl.multiple_of(i * 16 + p * 8, 8), 8)
            for j in range(key_heads):
                q = jnp.concatenate(
                    [
                        queries[
                            p * 8 : p * 8 + 8,
                            (j * group + g) * HEAD_SIZE : (j * group + g + 1) * HEAD_SIZE,
                        ]
                        for g in range(group)
                    ],
                    axis=0,
                ).astype(jnp.bfloat16)
                c = 2 * j * HEAD_SIZE
                k = page_ref[base : base + per_pair, :, c : c + HEAD_SIZE].reshape(keys, HEAD_SIZE)
                v = page_ref[base : base + per_pair, :, c + HEAD_SIZE : c + 2 * HEAD_SIZE]
                v = v.reshape(keys, HEAD_SIZE)
                s = lax.dot_general(q, k, NT, preferred_element_type=jnp.float32)
                s = jnp.where(visible, s, -jnp.inf)
                top = jnp.max(s, axis=1, keepdims=True)
                e = jnp.exp2((s - top) * SCALE2)
                total = jnp.sum(e, axis=1, keepdims=True)
                acc = jnp.dot(e.astype(jnp.bfloat16), v, preferred_element_type=jnp.float32)
                top = jnp.broadcast_to(top, acc.shape)
                total = jnp.broadcast_to(total, acc.shape)
                for g in range(group):
                    acc_ref[j, g, spot, :] = acc[g * 8 : g * 8 + 8]
                    top_ref[j, g, spot, :] = top[g * 8 : g * 8 + 8]
                    sum_ref[j, g, spot, :] = total[g * 8 : g * 8 + 8]

    @pl.when(i == page_steps)
    def _():
        for p in range(1, ranks):
            for c in range(own_chunks):
                x_transfer(p, c).wait()
        squares = jnp.zeros((tokens, 1), jnp.float32)
        for c in range(chunks):
            x = flat(x_all[c])
            squares += jnp.sum(x * x, axis=1, keepdims=True)
        inverse = lax.rsqrt(squares / (chunks * chunk) + epsilon)
        inverse_ref[...] = jnp.broadcast_to(inverse, inverse_ref.shape)

    @pl.when((i >= page_steps) & (i < page_steps + chunks))
    def _():
        c = i - page_steps
        scaled = (flat(x_all[c]) * inverse_ref[:, :1] * gain_ref[c]).astype(jnp.bfloat16)
        nk_sum[...] += jnp.dot(scaled, wk_ref[...], preferred_element_type=jnp.float32)
        nv_sum[...] += jnp.dot(scaled, wv_ref[...], preferred_element_type=jnp.float32)

    @pl.when(i == page_steps + chunks - 1)
    def _():
        nk = nk_sum[...].astype(jnp.bfloat16)
        nv = nv_sum[...].astype(jnp.bfloat16)
        for j in range(key_heads):
            nk_ref[j] = nk[:, j * HEAD_SIZE : (j + 1) * HEAD_SIZE]
            nv_ref[j] = nv[:, j * HEAD_SIZE : (j + 1) * HEAD_SIZE]

    def attend(j):
        keys = full[j, :, :HEAD_SIZE]
        values = full[j, :, HEAD_SIZE:]
        wide = 2
        row = lax.broadcasted_iota(jnp.int32, (wide * tokens, tokens), 0) % tokens
        col = lax.broadcasted_iota(jnp.int32, (wide * tokens, tokens), 1)
        visible = (row // steps == col // steps) & (col <= row)
        for g in range(0, group, wide):
            first = j * head_width + g * HEAD_SIZE
            q = jnp.concatenate(
                [
                    q_ref[:, first + w * HEAD_SIZE : first + (w + 1) * HEAD_SIZE]
                    for w in range(wide)
                ],
                axis=0,
            )
            paged = jnp.concatenate([acc_ref[j, g + w] for w in range(wide)], axis=0)
            paged_top = jnp.concatenate([top_ref[j, g + w][:, :1] for w in range(wide)], axis=0)
            paged_sum = jnp.concatenate([sum_ref[j, g + w][:, :1] for w in range(wide)], axis=0)
            s = lax.dot_general(q, keys, NT, preferred_element_type=jnp.float32)
            r = lax.dot_general(q, nk_ref[j], NT, preferred_element_type=jnp.float32)
            r = jnp.where(visible, r, -jnp.inf)
            top = jnp.maximum(jnp.max(s, axis=1, keepdims=True), jnp.max(r, axis=1, keepdims=True))
            top = jnp.maximum(top, paged_top)
            e = jnp.exp2((s - top) * SCALE2)
            f = jnp.exp2((r - top) * SCALE2)
            keep = jnp.exp2((paged_top - top) * SCALE2)
            total = (
                jnp.sum(e, axis=1, keepdims=True)
                + jnp.sum(f, axis=1, keepdims=True)
                + keep * paged_sum
            )
            acc = jnp.dot(e.astype(jnp.bfloat16), values, preferred_element_type=jnp.float32)
            acc += jnp.dot(f.astype(jnp.bfloat16), nv_ref[j], preferred_element_type=jnp.float32)
            acc = ((acc + keep * paged) / total).astype(jnp.bfloat16)
            both = jnp.concatenate([acc[w * tokens : (w + 1) * tokens] for w in range(wide)], axis=1)
            placed = jnp.dot(sel_ref[...], both, preferred_element_type=jnp.float32)
            outgoing[j, :, :, :, g * HEAD_SIZE : (g + wide) * HEAD_SIZE] = placed.reshape(
                members, CAP, steps, wide * HEAD_SIZE
            ).astype(jnp.bfloat16)

    for j in range(key_heads):

        @pl.when(i == page_steps + chunks + j)
        def _(j=j):
            attend(j)

            def send(p, carry):
                out_transfer(j, p).start()
                return carry

            lax.fori_loop(1, members, send, 0)
            own_out(j).start()

    for t in range(stages + key_heads - 1):
        if t < stages:
            when = t * (page_steps + chunks - 1) // (stages - 1)
        else:
            when = page_steps + chunks + t - stages

        @pl.when(i == when)
        def _(t=t):
            for j in range(key_heads):
                if 0 <= t - j < stages:
                    advance(t - j, j)

    @pl.when(i == final_step)
    def _():
        for j in range(key_heads):
            for k in range(stages):
                transfer(k, j).wait_send()

            def finish(p, carry):
                out_transfer(j, p).wait()
                return carry

            lax.fori_loop(1, members, finish, 0)
            own_out(j).wait()


def per_device(
    prefix_kv,
    page_key_values,
    context_len,
    prefill_owner,
    assign,
    x_new,
    norm_gain,
    key_weight,
    value_weight,
    decoded_queries,
):
    row_count, steps, width = decoded_queries.shape
    tokens = row_count * steps
    members = lax.axis_size("dp")
    ranks = lax.axis_size("tensor")
    levels = members.bit_length() - 1
    assigned = assign[:, 0]
    indices = jnp.arange(row_count)
    matching = (assigned[:, None] == assigned[None, :]) & (indices[None, :] < indices[:, None])
    ranking = jnp.sum(matching.astype(jnp.int32), axis=1)
    destination = assigned * CAP + ranking
    token_place = (destination[:, None] * steps + jnp.arange(steps)[None, :]).reshape(tokens)
    slots = members * CAP * steps
    selector = (jnp.arange(slots)[:, None] == token_place[None, :]).astype(jnp.bfloat16)

    length, kv_width = prefix_kv.shape
    span = page_key_values.shape[1]
    key_heads = kv_width // (2 * HEAD_SIZE)
    group = width // (key_heads * HEAD_SIZE)
    chunk = min(1024, width)
    chunks = ranks * width // chunk
    page_steps = tokens // 16
    new_width = key_weight.shape[1]

    def whole(*shape):
        return pl.BlockSpec(shape, lambda i: (0,) * len(shape))

    weight = pl.BlockSpec((chunk, new_width), lambda i: (jnp.clip(i - page_steps, 0, chunks - 1), 0))
    stat = pltpu.VMEM((key_heads, group, tokens, HEAD_SIZE), jnp.float32)
    decoded = pl.pallas_call(
        functools.partial(kernel, steps, levels, ranks),
        grid=(page_steps + chunks + key_heads,),
        in_specs=[
            pl.BlockSpec(memory_space=pltpu.SMEM),
            pl.BlockSpec(memory_space=pltpu.SMEM),
            whole(row_count, steps, width),
            pl.BlockSpec(
                (16 // steps, span, kv_width), lambda i: (jnp.minimum(i, page_steps - 1), 0, 0)
            ),
            whole(row_count, steps, width),
            whole(chunks, 1, chunk),
            weight,
            weight,
            whole(slots, tokens),
            pl.BlockSpec(memory_space=pl.ANY),
        ],
        out_specs=pl.BlockSpec(memory_space=pl.ANY),
        out_shape=jax.ShapeDtypeStruct((members * CAP, steps, width), jnp.bfloat16),
        scratch_shapes=[
            pltpu.VMEM((tokens, width), jnp.bfloat16),
            pltpu.VMEM((key_heads, length // 2, 2 * HEAD_SIZE), jnp.bfloat16),
            pltpu.VMEM((key_heads, length, 2 * HEAD_SIZE), jnp.bfloat16),
            pltpu.VMEM((chunks, row_count, steps, chunk), jnp.bfloat16),
            stat,
            stat,
            stat,
            pltpu.VMEM((tokens, new_width), jnp.float32),
            pltpu.VMEM((tokens, new_width), jnp.float32),
            pltpu.VMEM((tokens, HEAD_SIZE), jnp.float32),
            pltpu.VMEM((key_heads, tokens, HEAD_SIZE), jnp.bfloat16),
            pltpu.VMEM((key_heads, tokens, HEAD_SIZE), jnp.bfloat16),
            pltpu.VMEM((key_heads, members, CAP, steps, group * HEAD_SIZE), jnp.bfloat16),
            pltpu.SemaphoreType.DMA((key_heads,)),
            pltpu.SemaphoreType.DMA((2 * levels, key_heads)),
            pltpu.SemaphoreType.DMA((2 * levels, key_heads)),
            pltpu.SemaphoreType.DMA((ranks - 1, width // chunk)),
            pltpu.SemaphoreType.DMA((ranks - 1, width // chunk)),
            pltpu.SemaphoreType.DMA((key_heads, members)),
            pltpu.SemaphoreType.DMA((key_heads, members)),
            pltpu.SemaphoreType.DMA((key_heads,)),
        ]
        + [
            pltpu.VMEM((key_heads, length >> (b + 1), 2 * HEAD_SIZE), jnp.bfloat16)
            for b in range(levels)
        ],
        compiler_params=pltpu.CompilerParams(
            collective_id=0,
            has_side_effects=True,
            vmem_limit_bytes=VMEM_LIMIT,
            dimension_semantics=("arbitrary",),
        ),
        cost_estimate=pl.CostEstimate(
            flops=4 * tokens * length * width, bytes_accessed=2 * page_key_values.size, transcendentals=0
        ),
    )(
        context_len,
        prefill_owner,
        decoded_queries,
        page_key_values,
        x_new,
        norm_gain.reshape(chunks, 1, chunk),
        key_weight,
        value_weight,
        selector,
        prefix_kv,
    )
    return decoded


def solution(mesh):
    in_specs = (
        P("dp", "tensor"),
        P("dp", None, "tensor"),
        P("dp"),
        P(),
        P("dp", None),
        P("dp", None, "tensor"),
        P(),
        P(None, "tensor"),
        P(None, "tensor"),
        P("dp", None, "tensor"),
    )
    out_specs = P("dp", None, "tensor")
    return jax.shard_map(
        per_device, mesh=mesh, in_specs=in_specs, out_specs=out_specs, check_vma=False
    )
```

```python
import functools
import math

import jax
import jax.numpy as jnp
from jax import lax
from jax.experimental import pallas as pl
from jax.experimental.pallas import tpu as pltpu
from jax.sharding import PartitionSpec as P

HEAD_SIZE = 128
CAP = 2
epsilon = 1e-05
SCALE2 = math.log2(math.e) / math.sqrt(HEAD_SIZE)
VMEM_LIMIT = 56 * 1024 * 1024
NT = (((1,), (1,)), ((), ()))


def bit(index, b):
    return (index // 2**b) % 2


def kernel(
    steps,
    levels,
    ranks,
    len_ref,
    owner_ref,
    q_in,
    page_ref,
    x_ref,
    gain_ref,
    wk_ref,
    wv_ref,
    sel_ref,
    prefix_ref,
    out_ref,
    q_ref,
    work,
    full,
    x_all,
    acc_ref,
    top_ref,
    sum_ref,
    nk_sum,
    nv_sum,
    inverse_ref,
    nk_ref,
    nv_ref,
    outgoing,
    copy_sem,
    send_sem,
    recv_sem,
    x_send,
    x_recv,
    o_send,
    o_recv,
    own_sem,
    *landing,
):
    i = pl.program_id(0)
    me = lax.axis_index("dp")
    rank = lax.axis_index("tensor")
    members = 2**levels
    tokens, width = q_ref.shape
    length = prefix_ref.shape[0]
    key_heads = work.shape[0]
    group = width // (key_heads * HEAD_SIZE)
    span = page_ref.shape[1]
    page_steps = tokens // 16
    chunks, _, chunk = gain_ref.shape
    own_chunks = chunks // ranks
    head_width = group * HEAD_SIZE
    final_step = page_steps + chunks + key_heads - 1
    stages = 2 * levels

    def flat(block):
        return block.astype(jnp.float32).reshape(tokens, block.shape[-1])

    def low(b, first):
        start = 0
        for a in range(first, b + 1):
            start = start + bit(me, a) * (length >> (a + 1))
        return start

    def rows(start, size):
        return pl.ds(pl.multiple_of(start, size), size)

    def transfer(k, j):
        if k < levels:
            b = k
            size = length >> (b + 1)
            if b == 0:
                start = (1 - bit(me, 0)) * size
                source = prefix_ref.at[rows(start, size), j * 2 * HEAD_SIZE : (j + 1) * 2 * HEAD_SIZE]
            else:
                start = low(b - 1, 1) + (1 - bit(me, b)) * size
                source = work.at[j, rows(start, size), :]
            target = landing[b].at[j]
        else:
            b = stages - 1 - k
            size = length >> (b + 1)
            source = full.at[j, rows(low(b, 0), size), :]
            target = source
        partner = me + (1 - 2 * bit(me, b)) * 2**b
        return pltpu.make_async_remote_copy(
            src_ref=source,
            dst_ref=target,
            send_sem=send_sem.at[k, j],
            recv_sem=recv_sem.at[k, j],
            device_id={"dp": partner},
            device_id_type=pl.DeviceIdType.MESH,
        )

    def kept(j):
        size = length // 2
        return pltpu.make_async_copy(
            prefix_ref.at[rows(bit(me, 0) * size, size), j * 2 * HEAD_SIZE : (j + 1) * 2 * HEAD_SIZE],
            work.at[j],
            copy_sem.at[j],
        )

    def x_transfer(p, c):
        peer = lax.rem(rank + p, ranks)
        return pltpu.make_async_remote_copy(
            src_ref=x_ref.at[:, :, c * chunk : (c + 1) * chunk],
            dst_ref=x_all.at[rank * own_chunks + c],
            send_sem=x_send.at[p - 1, c],
            recv_sem=x_recv.at[p - 1, c],
            device_id={"tensor": peer},
            device_id_type=pl.DeviceIdType.MESH,
        )

    def out_transfer(j, p):
        dest = lax.rem(me + p, members)
        return pltpu.make_async_remote_copy(
            src_ref=outgoing.at[j, dest],
            dst_ref=out_ref.at[pl.ds(me * CAP, CAP), :, j * head_width : (j + 1) * head_width],
            send_sem=o_send.at[j, p],
            recv_sem=o_recv.at[j, p],
            device_id={"dp": dest},
            device_id_type=pl.DeviceIdType.MESH,
        )

    def own_out(j):
        return pltpu.make_async_copy(
            outgoing.at[j, me],
            out_ref.at[pl.ds(me * CAP, CAP), :, j * head_width : (j + 1) * head_width],
            own_sem.at[j],
        )

    def advance(k, j):
        transfer(k, j).wait_recv()
        if k < levels:
            b = k
            size = length >> (b + 1)
            if b == 0:
                kept(j).wait()
            span_rows = rows(low(b, 1), size)
            mine = work[j, span_rows, :]
            other = landing[b][j]
            side = jnp.zeros(mine.shape, jnp.int32) + owner_ref[0]
            away = ((side // 2**b) % 2 - bit(me, b)).astype(jnp.float32)
            away = (away * away).astype(jnp.bfloat16)
            merged = mine * (1 - away) + other * away
            if b < levels - 1:
                work[j, span_rows, :] = merged
            else:
                full[j, rows(low(b, 0), size), :] = merged
        if k < stages - 1:
            transfer(k + 1, j).start()

    @pl.when(i == 0)
    def _():
        barrier = pltpu.get_barrier_semaphore()

        def greet(p, carry):
            pl.semaphore_signal(
                barrier,
                inc=1,
                device_id={"dp": lax.rem(me + p, members)},
                device_id_type=pl.DeviceIdType.MESH,
            )
            return carry

        lax.fori_loop(1, members, greet, 0)
        for p in range(1, ranks):
            pl.semaphore_signal(
                barrier,
                inc=1,
                device_id={"tensor": lax.rem(rank + p, ranks)},
                device_id_type=pl.DeviceIdType.MESH,
            )
        for j in range(key_heads):
            kept(j).start()
        pl.semaphore_wait(barrier, members - 1 + ranks - 1)
        for j in range(key_heads):
            transfer(0, j).start()
        for p in range(1, ranks):
            for c in range(own_chunks):
                x_transfer(p, c).start()
        for c in range(own_chunks):
            x_all[rank * own_chunks + c] = x_ref[:, :, c * chunk : (c + 1) * chunk]
        for c in range(own_chunks):
            q_ref[:, c * chunk : (c + 1) * chunk] = flat(
                q_in[:, :, c * chunk : (c + 1) * chunk]
            ).astype(jnp.bfloat16)
        nk_sum[...] = jnp.zeros_like(nk_sum)
        nv_sum[...] = jnp.zeros_like(nv_sum)

    @pl.when(i < page_steps)
    def _():
        per_pair = 8 // steps
        queries = q_ref[pl.ds(pl.multiple_of(i * 16, 16), 16), :].astype(jnp.float32)
        count = group * 8
        keys = per_pair * span
        row = lax.broadcasted_iota(jnp.int32, (count, keys), 0)
        col = lax.broadcasted_iota(jnp.int32, (count, keys), 1)
        holder = (row % 8) // steps
        for p in range(2):
            limit = jnp.zeros((count, keys), jnp.int32)
            for k in range(per_pair):
                used = len_ref[i * (16 // steps) + p * per_pair + k]
                limit = jnp.where(holder == k, used, limit)
            place = col - holder * span
            visible = (place >= 0) & (place < limit)
            base = p * per_pair
            spot = pl.ds(pl.multiple_of(i * 16 + p * 8, 8), 8)
            for j in range(key_heads):
                q = jnp.concatenate(
                    [
                        queries[
                            p * 8 : p * 8 + 8,
                            (j * group + g) * HEAD_SIZE : (j * group + g + 1) * HEAD_SIZE,
                        ]
                        for g in range(group)
                    ],
                    axis=0,
                ).astype(jnp.bfloat16)
                c = 2 * j * HEAD_SIZE
                k = page_ref[base : base + per_pair, :, c : c + HEAD_SIZE].reshape(keys, HEAD_SIZE)
                v = page_ref[base : base + per_pair, :, c + HEAD_SIZE : c + 2 * HEAD_SIZE]
                v = v.reshape(keys, HEAD_SIZE)
                s = lax.dot_general(q, k, NT, preferred_element_type=jnp.float32)
                s = jnp.where(visible, s, -jnp.inf)
                top = jnp.max(s, axis=1, keepdims=True)
                e = jnp.exp2((s - top) * SCALE2)
                total = jnp.sum(e, axis=1, keepdims=True)
                acc = jnp.dot(e.astype(jnp.bfloat16), v, preferred_element_type=jnp.float32)
                top = jnp.broadcast_to(top, acc.shape)
                total = jnp.broadcast_to(total, acc.shape)
                for g in range(group):
                    acc_ref[j, g, spot, :] = acc[g * 8 : g * 8 + 8]
                    top_ref[j, g, spot, :] = top[g * 8 : g * 8 + 8]
                    sum_ref[j, g, spot, :] = total[g * 8 : g * 8 + 8]

    @pl.when(i == page_steps)
    def _():
        for p in range(1, ranks):
            for c in range(own_chunks):
                x_transfer(p, c).wait()
        squares = jnp.zeros((tokens, 1), jnp.float32)
        for c in range(chunks):
            x = flat(x_all[c])
            squares += jnp.sum(x * x, axis=1, keepdims=True)
        inverse = lax.rsqrt(squares / (chunks * chunk) + epsilon)
        inverse_ref[...] = jnp.broadcast_to(inverse, inverse_ref.shape)

    @pl.when((i >= page_steps) & (i < page_steps + chunks))
    def _():
        c = i - page_steps
        scaled = (flat(x_all[c]) * inverse_ref[:, :1] * gain_ref[c]).astype(jnp.bfloat16)
        nk_sum[...] += jnp.dot(scaled, wk_ref[...], preferred_element_type=jnp.float32)
        nv_sum[...] += jnp.dot(scaled, wv_ref[...], preferred_element_type=jnp.float32)

    @pl.when(i == page_steps + chunks - 1)
    def _():
        nk = nk_sum[...].astype(jnp.bfloat16)
        nv = nv_sum[...].astype(jnp.bfloat16)
        for j in range(key_heads):
            nk_ref[j] = nk[:, j * HEAD_SIZE : (j + 1) * HEAD_SIZE]
            nv_ref[j] = nv[:, j * HEAD_SIZE : (j + 1) * HEAD_SIZE]

    def attend(j):
        keys = full[j, :, :HEAD_SIZE]
        values = full[j, :, HEAD_SIZE:]
        wide = 2
        row = lax.broadcasted_iota(jnp.int32, (wide * tokens, tokens), 0) % tokens
        col = lax.broadcasted_iota(jnp.int32, (wide * tokens, tokens), 1)
        visible = (row // steps == col // steps) & (col <= row)
        for g in range(0, group, wide):
            first = j * head_width + g * HEAD_SIZE
            q = jnp.concatenate(
                [
                    q_ref[:, first + w * HEAD_SIZE : first + (w + 1) * HEAD_SIZE]
                    for w in range(wide)
                ],
                axis=0,
            )
            paged = jnp.concatenate([acc_ref[j, g + w] for w in range(wide)], axis=0)
            paged_top = jnp.concatenate([top_ref[j, g + w][:, :1] for w in range(wide)], axis=0)
            paged_sum = jnp.concatenate([sum_ref[j, g + w][:, :1] for w in range(wide)], axis=0)
            s = lax.dot_general(q, keys, NT, preferred_element_type=jnp.float32)
            r = lax.dot_general(q, nk_ref[j], NT, preferred_element_type=jnp.float32)
            r = jnp.where(visible, r, -jnp.inf)
            top = jnp.maximum(jnp.max(s, axis=1, keepdims=True), jnp.max(r, axis=1, keepdims=True))
            top = jnp.maximum(top, paged_top)
            e = jnp.exp2((s - top) * SCALE2)
            f = jnp.exp2((r - top) * SCALE2)
            keep = jnp.exp2((paged_top - top) * SCALE2)
            total = (
                jnp.sum(e, axis=1, keepdims=True)
                + jnp.sum(f, axis=1, keepdims=True)
                + keep * paged_sum
            )
            acc = jnp.dot(e.astype(jnp.bfloat16), values, preferred_element_type=jnp.float32)
            acc += jnp.dot(f.astype(jnp.bfloat16), nv_ref[j], preferred_element_type=jnp.float32)
            acc = ((acc + keep * paged) / total).astype(jnp.bfloat16)
            both = jnp.concatenate([acc[w * tokens : (w + 1) * tokens] for w in range(wide)], axis=1)
            placed = jnp.dot(sel_ref[...], both, preferred_element_type=jnp.float32)
            outgoing[j, :, :, :, g * HEAD_SIZE : (g + wide) * HEAD_SIZE] = placed.reshape(
                members, CAP, steps, wide * HEAD_SIZE
            ).astype(jnp.bfloat16)

    for j in range(key_heads):

        @pl.when(i == page_steps + chunks + j)
        def _(j=j):
            attend(j)

            def send(p, carry):
                out_transfer(j, p).start()
                return carry

            lax.fori_loop(1, members, send, 0)
            own_out(j).start()

    for t in range(stages + key_heads - 1):
        if t < stages:
            when = t * (page_steps + chunks - 1) // (stages - 1)
        else:
            when = page_steps + chunks + t - stages

        @pl.when(i == when)
        def _(t=t):
            late = t - (stages - 2)
            if t >= stages:
                advance(stages - 2, late - 1)
            for j in reversed(range(key_heads)):
                if 0 <= t - j < stages and not (t >= stages - 1 and j == late):
                    advance(t - j, j)

    @pl.when(i == final_step)
    def _():
        for j in range(key_heads):
            for k in range(stages):
                transfer(k, j).wait_send()

            def finish(p, carry):
                out_transfer(j, p).wait()
                return carry

            lax.fori_loop(1, members, finish, 0)
            own_out(j).wait()


def per_device(
    prefix_kv,
    page_key_values,
    context_len,
    prefill_owner,
    assign,
    x_new,
    norm_gain,
    key_weight,
    value_weight,
    decoded_queries,
):
    row_count, steps, width = decoded_queries.shape
    tokens = row_count * steps
    members = lax.axis_size("dp")
    ranks = lax.axis_size("tensor")
    levels = members.bit_length() - 1
    assigned = assign[:, 0]
    indices = jnp.arange(row_count)
    matching = (assigned[:, None] == assigned[None, :]) & (indices[None, :] < indices[:, None])
    ranking = jnp.sum(matching.astype(jnp.int32), axis=1)
    destination = assigned * CAP + ranking
    token_place = (destination[:, None] * steps + jnp.arange(steps)[None, :]).reshape(tokens)
    slots = members * CAP * steps
    selector = (jnp.arange(slots)[:, None] == token_place[None, :]).astype(jnp.bfloat16)

    length, kv_width = prefix_kv.shape
    span = page_key_values.shape[1]
    key_heads = kv_width // (2 * HEAD_SIZE)
    group = width // (key_heads * HEAD_SIZE)
    chunk = min(1024, width)
    chunks = ranks * width // chunk
    page_steps = tokens // 16
    new_width = key_weight.shape[1]

    def whole(*shape):
        return pl.BlockSpec(shape, lambda i: (0,) * len(shape))

    weight = pl.BlockSpec((chunk, new_width), lambda i: (jnp.clip(i - page_steps, 0, chunks - 1), 0))
    stat = pltpu.VMEM((key_heads, group, tokens, HEAD_SIZE), jnp.float32)
    decoded = pl.pallas_call(
        functools.partial(kernel, steps, levels, ranks),
        grid=(page_steps + chunks + key_heads,),
        in_specs=[
            pl.BlockSpec(memory_space=pltpu.SMEM),
            pl.BlockSpec(memory_space=pltpu.SMEM),
            whole(row_count, steps, width),
            pl.BlockSpec(
                (16 // steps, span, kv_width), lambda i: (jnp.minimum(i, page_steps - 1), 0, 0)
            ),
            whole(row_count, steps, width),
            whole(chunks, 1, chunk),
            weight,
            weight,
            whole(slots, tokens),
            pl.BlockSpec(memory_space=pl.ANY),
        ],
        out_specs=pl.BlockSpec(memory_space=pl.ANY),
        out_shape=jax.ShapeDtypeStruct((members * CAP, steps, width), jnp.bfloat16),
        scratch_shapes=[
            pltpu.VMEM((tokens, width), jnp.bfloat16),
            pltpu.VMEM((key_heads, length // 2, 2 * HEAD_SIZE), jnp.bfloat16),
            pltpu.VMEM((key_heads, length, 2 * HEAD_SIZE), jnp.bfloat16),
            pltpu.VMEM((chunks, row_count, steps, chunk), jnp.bfloat16),
            stat,
            stat,
            stat,
            pltpu.VMEM((tokens, new_width), jnp.float32),
            pltpu.VMEM((tokens, new_width), jnp.float32),
            pltpu.VMEM((tokens, HEAD_SIZE), jnp.float32),
            pltpu.VMEM((key_heads, tokens, HEAD_SIZE), jnp.bfloat16),
            pltpu.VMEM((key_heads, tokens, HEAD_SIZE), jnp.bfloat16),
            pltpu.VMEM((key_heads, members, CAP, steps, group * HEAD_SIZE), jnp.bfloat16),
            pltpu.SemaphoreType.DMA((key_heads,)),
            pltpu.SemaphoreType.DMA((2 * levels, key_heads)),
            pltpu.SemaphoreType.DMA((2 * levels, key_heads)),
            pltpu.SemaphoreType.DMA((ranks - 1, width // chunk)),
            pltpu.SemaphoreType.DMA((ranks - 1, width // chunk)),
            pltpu.SemaphoreType.DMA((key_heads, members)),
            pltpu.SemaphoreType.DMA((key_heads, members)),
            pltpu.SemaphoreType.DMA((key_heads,)),
        ]
        + [
            pltpu.VMEM((key_heads, length >> (b + 1), 2 * HEAD_SIZE), jnp.bfloat16)
            for b in range(levels)
        ],
        compiler_params=pltpu.CompilerParams(
            collective_id=0,
            has_side_effects=True,
            vmem_limit_bytes=VMEM_LIMIT,
            dimension_semantics=("arbitrary",),
        ),
        cost_estimate=pl.CostEstimate(
            flops=4 * tokens * length * width, bytes_accessed=2 * page_key_values.size, transcendentals=0
        ),
    )(
        context_len,
        prefill_owner,
        decoded_queries,
        page_key_values,
        x_new,
        norm_gain.reshape(chunks, 1, chunk),
        key_weight,
        value_weight,
        selector,
        prefix_kv,
    )
    return decoded


def solution(mesh):
    in_specs = (
        P("dp", "tensor"),
        P("dp", None, "tensor"),
        P("dp"),
        P(),
        P("dp", None),
        P("dp", None, "tensor"),
        P(),
        P(None, "tensor"),
        P(None, "tensor"),
        P("dp", None, "tensor"),
    )
    out_specs = P("dp", None, "tensor")
    return jax.shard_map(
        per_device, mesh=mesh, in_specs=in_specs, out_specs=out_specs, check_vma=False
    )
```
